32 devices in a mesh: groups: 2 (over x), blk: 16 (over z, y, core).
Axes of the slice: x: 2, y: 2, z: 4, core: 2. Of those that a mesh axis runs over, the one named last changes fastest.
Arguments:
- student: bfloat16 [12288, 1024], P(('groups', 'blk')), parts along dimension 0, may hold values from -60 to 60
- teacher: bfloat16 [12288, 4096], P(('groups', 'blk')), parts along dimension 0, may hold values from -60 to 60
Outputs:
- student_grad: float32 [12288, 1024], P(('groups', 'blk')), parts along dimension 0
The draws below stay inside these ranges and needn't reach their ends.
There are 2 independent parts, one for each index of `groups`. The reference program is written for one: setup_inputs(seed, part) draws one part's arguments, and reference() takes and returns one part's arrays. A program takes and returns all parts, laid end to end along the dimension named above; each array names one. Nothing has to cross between parts.
All inputs are finite; a program needn't handle non-finite values.
Results may differ from the reference program's by a relative error of at most 0.0085.
Values may be sent and summed in bfloat16 or wider, within the bound.
A program may use at most 64 MiB of HBM per device.

```python
import math
import jax
import jax.numpy as jnp
from jax import lax

DS = 1024
DT = 4096
ROWS_DEV = 384
HOPS = 4
SENTENCES = 6144


def spread_rows(noise, row_key, top, base):
    rows = jnp.exp(jax.random.uniform(row_key, (noise.shape[0], 1), jnp.float32) * math.log(top))
    return (noise * rows * base).astype(jnp.bfloat16)


def draw_student(key, part):
    key = jax.random.fold_in(key, 11)
    first, second = jax.random.split(key, 2)
    noise = jnp.clip(jax.random.normal(first, (SENTENCES, DS), jnp.float32), -5.0, 5.0)
    top = 10.0
    return spread_rows(noise, second, top, 0.5 / math.sqrt(DS))


def draw_teacher(key, part):
    key = jax.random.fold_in(key, 23)
    first, second = jax.random.split(key, 2)
    noise = jnp.clip(jax.random.normal(first, (SENTENCES, DT), jnp.float32), -5.0, 5.0)
    top = 10.0
    return spread_rows(noise, second, top, 0.5 / math.sqrt(DT))


def setup_inputs(seed: int = 0, part: int = 0) -> dict:
    splits = jax.random.split(jax.random.key(seed), 3)
    own_keys = jax.random.split(jax.random.fold_in(splits[2], part), 3)
    return {
        "student": draw_student(jax.random.fold_in(jax.random.fold_in(splits[2], part), 71), part),
        "teacher": draw_teacher(jax.random.fold_in(jax.random.fold_in(splits[2], part), 71), part),
    }


SIM_SCALE = 32.0

def unit_rows(rows):
    values = rows.astype(jnp.float32)
    length = jnp.sqrt(lax.optimization_barrier(jnp.sum(values * values, axis=1, keepdims=True)) + 1e-12)
    return ((values / length).astype(jnp.bfloat16), length)

def contract_rows(left, right):
    return lax.dot_general(left, right, (((1,), (1,)), ((), ())), preferred_element_type=jnp.float32)

def finish(unit_grad, unit_stu, stu_len):
    unit_float = unit_stu.astype(jnp.float32)
    radial = lax.optimization_barrier(jnp.sum(unit_float * unit_grad, axis=1, keepdims=True))
    return (unit_grad - unit_float * radial) / stu_len

def reference(student, teacher):
    unit_stu, stu_len = unit_rows(student)
    unit_tea, _ = unit_rows(teacher)
    count = student.shape[0]
    blocks = count // ROWS_DEV
    stu_blocks = unit_stu.reshape(blocks, ROWS_DEV, DS)
    tea_blocks = unit_tea.reshape(blocks, ROWS_DEV, DT)
    offsets = jnp.arange(-HOPS, HOPS + 1, dtype=jnp.int32)

    def one_block(index):
        near = (index + offsets + blocks) % blocks
        band_stu = jnp.take(stu_blocks, near, axis=0).reshape(-1, DS)
        band_tea = jnp.take(tea_blocks, near, axis=0).reshape(-1, DT)
        own_stu = stu_blocks[index]
        own_tea = tea_blocks[index]
        diff = contract_rows(own_stu, band_stu) - contract_rows(own_tea, band_tea)
        contrast = (SIM_SCALE * diff).astype(jnp.bfloat16)
        return jnp.dot(contrast, band_stu, preferred_element_type=jnp.float32)
    sums = lax.map(one_block, jnp.arange(blocks, dtype=jnp.int32)).reshape(count, DS)
    unit_grad = 2.0 * SIM_SCALE / count * sums
    return finish(unit_grad, unit_stu, stu_len)
```

```python
import functools

import jax
import jax.numpy as jnp
from jax import lax
from jax.experimental import pallas as pl
from jax.experimental.pallas import tpu as pltpu
from jax.sharding import PartitionSpec as P

SIM_SCALE = 32.0
CHUNK = 64
MESH = pl.DeviceIdType.MESH

ROWS_A, ROWS_B, ROWS_C, ROWS_D, GRAD_CD, GRAD_B, GRAD_A = range(7)


def kernel(
    n, chunk, stu_ref, tea_ref, out_ref,
    own, neg, buf, acc, length, part_a, cd_out, cd_in, b_out, b_in, a_out, a_in, send, recv,
):
    rows, ds = stu_ref.shape
    steps = rows // chunk
    me = lax.axis_index("blk")
    core = lax.rem(me, 2)
    half = lax.rem(lax.div(me, 2), 2)
    up = lax.rem(me + 4, n)
    down = lax.rem(me + n - 4, n)
    side = me + 2 - 4 * half
    mate = me + 1 - 2 * core

    def part(c):
        return pl.ds(pl.multiple_of(c * chunk, chunk), chunk)

    def slot(c, kind):
        return buf.at[c, pl.ds(kind * chunk, chunk)]

    def copy(kind, c, src, dst, to):
        return pltpu.make_async_remote_copy(
            src_ref=src, dst_ref=dst, send_sem=send.at[kind, c], recv_sem=recv.at[kind, c],
            device_id={"blk": to}, device_id_type=MESH,
        )

    def rows_copy(kind, c, src):
        to = (up, side, mate, mate)[kind]
        return copy(kind, c, src, slot(c, kind), to)

    def grad_copy(kind, c):
        src, dst, to = {
            GRAD_CD: (cd_out, cd_in, mate),
            GRAD_B: (b_out, b_in, side),
            GRAD_A: (a_out, a_in, down),
        }[kind]
        return copy(kind, c, src.at[c], dst.at[c], to)

    barrier = pltpu.get_barrier_semaphore()
    for other in (up, down, side, mate):
        pl.semaphore_signal(barrier, inc=1, device_id={"blk": other}, device_id_type=MESH)

    def normalise(c):
        stu = stu_ref[part(c), :].astype(jnp.float32)
        stu_len = jnp.sqrt(jnp.sum(stu * stu, axis=1, keepdims=True) + 1e-12)
        unit = (stu * (1.0 / stu_len)).astype(jnp.bfloat16)
        length[part(c), :] = stu_len
        own[part(c), :ds] = unit
        neg[part(c), :ds] = unit
        tea = tea_ref[part(c), :].astype(jnp.float32)
        tea_len = jnp.sqrt(jnp.sum(tea * tea, axis=1, keepdims=True) + 1e-12)
        unit = (tea * (1.0 / tea_len)).astype(jnp.bfloat16)
        own[part(c), ds:] = unit
        neg[part(c), ds:] = -unit

    normalise(0)
    pl.semaphore_wait(barrier, 4)

    @pl.loop(0, steps)
    def _(c):
        mine = own.at[part(c)]
        rows_copy(ROWS_A, c, mine).start()

        @pl.when(half == 0)
        def _():
            rows_copy(ROWS_B, c, mine).start()

        @pl.when(core == 0)
        def _():
            rows_copy(ROWS_D, c, mine).start()

        @pl.when(c + 1 < steps)
        def _():
            normalise(c + 1)

    def gram_tile(far):
        gram = lax.dot_general(
            neg[...], far, (((1,), (1,)), ((), ())), preferred_element_type=jnp.float32
        )
        return (SIM_SCALE * gram).astype(jnp.bfloat16)

    acc[...] = jnp.dot(
        gram_tile(own[...]), own[:, :ds], preferred_element_type=jnp.float32
    )

    def return_a(c):
        grad_copy(GRAD_B, c).wait_recv()
        total = part_a[c]
        total += jnp.where(core == 1, cd_in[c, chunk:, :].astype(jnp.float32), 0.0)
        total += jnp.where(half == 1, b_in[c].astype(jnp.float32), 0.0)
        a_out[c] = total.astype(jnp.bfloat16)
        grad_copy(GRAD_A, c).start()

    @pl.loop(0, steps)
    def _(c):
        arrived = slot(c, ROWS_A)
        rows_copy(ROWS_A, c, arrived).wait_recv()

        @pl.when(half == 1)
        def _():
            rows_copy(ROWS_B, c, arrived).start()

        @pl.when(core == 1)
        def _():
            rows_copy(ROWS_D, c, arrived).start()

        second = slot(c, ROWS_B)
        rows_copy(ROWS_B, c, second).wait_recv()
        rows_copy(ROWS_C, c, second).start()
        rows_copy(ROWS_D, c, second).wait_recv()
        rows_copy(ROWS_C, c, second).wait_recv()

        tile = gram_tile(buf[c])
        terms = lax.dot_general(
            tile, own[:, :ds], (((0,), (0,)), ((), ())), preferred_element_type=jnp.float32
        )
        cd_out[c] = terms[2 * chunk :, :].astype(jnp.bfloat16)
        grad_copy(GRAD_CD, c).start()
        part_a[c] = terms[:chunk, :]
        term_b = terms[chunk : 2 * chunk, :]
        acc[...] += jnp.dot(tile, buf[c, :, :ds], preferred_element_type=jnp.float32)
        grad_copy(GRAD_CD, c).wait_recv()
        b_out[c] = (term_b + cd_in[c, :chunk, :].astype(jnp.float32)).astype(jnp.bfloat16)
        grad_copy(GRAD_B, c).start()

        @pl.when(c > 0)
        def _():
            return_a(c - 1)

    return_a(steps - 1)

    @pl.loop(0, steps)
    def _(c):
        grad_copy(GRAD_A, c).wait_recv()
        total = acc[part(c), :] + a_in[c].astype(jnp.float32)
        total += jnp.where(core == 0, cd_in[c, chunk:, :].astype(jnp.float32), 0.0)
        total += jnp.where(half == 0, b_in[c].astype(jnp.float32), 0.0)
        grad = 2.0 * SIM_SCALE / (rows * n) * total
        unit = own[part(c), :ds].astype(jnp.float32)
        radial = jnp.sum(unit * grad, axis=1, keepdims=True)
        out_ref[part(c), :] = (grad - unit * radial) / length[part(c), :]

    @pl.loop(0, steps)
    def _(c):
        for kind in (ROWS_A, ROWS_B, ROWS_C, ROWS_D):
            rows_copy(kind, c, own.at[part(c)]).wait_send()
        for kind in (GRAD_CD, GRAD_B, GRAD_A):
            grad_copy(kind, c).wait_send()


def body(student, teacher):
    rows, ds = student.shape
    dt = teacher.shape[1]
    n = lax.axis_size("blk")
    chunk = CHUNK
    steps = rows // chunk
    wide = ds + dt
    bf16, f32 = jnp.bfloat16, jnp.float32
    flops = 2 * rows * rows * (5 * wide + 9 * ds)
    return pl.pallas_call(
        functools.partial(kernel, n, chunk),
        out_shape=jax.ShapeDtypeStruct((rows, ds), f32),
        in_specs=[pl.BlockSpec(memory_space=pltpu.VMEM)] * 2,
        out_specs=pl.BlockSpec(memory_space=pltpu.VMEM),
        scratch_shapes=[
            pltpu.VMEM((rows, wide), bf16),
            pltpu.VMEM((rows, wide), bf16),
            pltpu.VMEM((steps, 4 * chunk, wide), bf16),
            pltpu.VMEM((rows, ds), f32),
            pltpu.VMEM((rows, 1), f32),
            pltpu.VMEM((steps, chunk, ds), f32),
            pltpu.VMEM((steps, 2 * chunk, ds), bf16),
            pltpu.VMEM((steps, 2 * chunk, ds), bf16),
            pltpu.VMEM((steps, chunk, ds), bf16),
            pltpu.VMEM((steps, chunk, ds), bf16),
            pltpu.VMEM((steps, chunk, ds), bf16),
            pltpu.VMEM((steps, chunk, ds), bf16),
            pltpu.SemaphoreType.DMA((7, steps)),
            pltpu.SemaphoreType.DMA((7, steps)),
        ],
        compiler_params=pltpu.CompilerParams(
            collective_id=0, has_side_effects=True, vmem_limit_bytes=56 * 1024 * 1024
        ),
        cost_estimate=pl.CostEstimate(
            flops=flops, bytes_accessed=2 * rows * wide + 4 * rows * ds, transcendentals=0
        ),
    )(student, teacher)


def solution(mesh):
    placed = (P(("groups", "blk"), None), P(("groups", "blk"), None))
    return jax.shard_map(
        body, mesh=mesh, in_specs=placed, out_specs=P(("groups", "blk"), None), check_vma=False
    )
```

```python
import functools

import jax
import jax.numpy as jnp
from jax import lax
from jax.experimental import pallas as pl
from jax.experimental.pallas import tpu as pltpu
from jax.sharding import PartitionSpec as P

SIM_SCALE = 32.0
CHUNK = 64
PIECE = 16
WINDOW = 3
LAG = 2
MESH = pl.DeviceIdType.MESH

ROWS_A, ROWS_B, ROWS_C, ROWS_D, GRAD_CD, GRAD_B, GRAD_A = range(7)


def kernel(
    n, chunk, piece, stu_ref, tea_ref, out_ref,
    own, neg, buf, acc, length, part_ab, cd_out, cd_in, b_out, b_in, a_out, a_in, send, recv,
):
    rows, ds = stu_ref.shape
    steps = rows // chunk
    pieces = rows // piece
    per = chunk // piece
    me = lax.axis_index("blk")
    core = lax.rem(me, 2)
    half = lax.rem(lax.div(me, 2), 2)
    up = lax.rem(me + 4, n)
    down = lax.rem(me + n - 4, n)
    side = me + 2 - 4 * half
    mate = me + 1 - 2 * core

    def part(c):
        return pl.ds(pl.multiple_of(c * chunk, chunk), chunk)

    def small(g):
        return pl.ds(pl.multiple_of(g * piece, piece), piece)

    def slot(g, kind):
        start = kind * chunk + lax.rem(g, per) * piece
        return buf.at[lax.div(g, per), pl.ds(pl.multiple_of(start, piece), piece)]

    def copy(kind, c, src, dst, to):
        return pltpu.make_async_remote_copy(
            src_ref=src, dst_ref=dst, send_sem=send.at[kind, c], recv_sem=recv.at[kind, c],
            device_id={"blk": to}, device_id_type=MESH,
        )

    def rows_copy(kind, g, src):
        to = (up, side, mate, mate)[kind]
        return copy(kind, g, src, slot(g, kind), to)

    def sent(kind, g):
        rows_copy(kind, g, own.at[small(g)]).wait_send()

    def arrived(kind, g):
        rows_copy(kind, g, own.at[small(g)]).wait_recv()

    def grad_copy(kind, c):
        src, dst, to = {
            GRAD_CD: (cd_out, cd_in, mate),
            GRAD_B: (b_out, b_in, side),
            GRAD_A: (a_out, a_in, down),
        }[kind]
        return copy(kind, c, src.at[c], dst.at[c], to)

    barrier = pltpu.get_barrier_semaphore()
    for other in (up, down, side, mate):
        pl.semaphore_signal(barrier, inc=1, device_id={"blk": other}, device_id_type=MESH)

    def normalise(g):
        here = small(g)
        stu = stu_ref[here, :].astype(jnp.float32)
        stu_len = jnp.sqrt(jnp.sum(stu * stu, axis=1, keepdims=True) + 1e-12)
        unit = (stu * (1.0 / stu_len)).astype(jnp.bfloat16)
        length[here, :] = stu_len
        own[here, :ds] = unit
        neg[here, :ds] = unit
        tea = tea_ref[here, :].astype(jnp.float32)
        tea_len = jnp.sqrt(jnp.sum(tea * tea, axis=1, keepdims=True) + 1e-12)
        unit = (tea * (1.0 / tea_len)).astype(jnp.bfloat16)
        own[here, ds:] = unit
        neg[here, ds:] = -unit

    def send_own(g):
        mine = own.at[small(g)]
        rows_copy(ROWS_A, g, mine).start()

        @pl.when(half == 0)
        def _():
            rows_copy(ROWS_B, g, mine).start()

        @pl.when(core == 0)
        def _():
            rows_copy(ROWS_D, g, mine).start()

    normalise(0)
    pl.semaphore_wait(barrier, 4)

    @pl.loop(0, pieces)
    def _(g):
        @pl.when(g > 0)
        def _():
            normalise(g)

        @pl.when(g < WINDOW)
        def _():
            send_own(g)

    def gram_tile(far):
        gram = lax.dot_general(
            neg[...], far, (((1,), (1,)), ((), ())), preferred_element_type=jnp.float32
        )
        return (SIM_SCALE * gram).astype(jnp.bfloat16)

    def own_tile():
        acc[...] = jnp.dot(
            gram_tile(own[...]), own[:, :ds], preferred_element_type=jnp.float32
        )

    def forward_first(g):
        arrived(ROWS_A, g)

        @pl.when(half == 1)
        def _():
            rows_copy(ROWS_B, g, slot(g, ROWS_A)).start()

        @pl.when(core == 1)
        def _():
            rows_copy(ROWS_D, g, slot(g, ROWS_A)).start()

    def forward_second(g):
        arrived(ROWS_B, g)
        rows_copy(ROWS_C, g, slot(g, ROWS_B)).start()

    def next_own(g):
        sent(ROWS_A, g)

        @pl.when(half == 0)
        def _():
            sent(ROWS_B, g)

        send_own(g + WINDOW)

    def tiles(c):
        @pl.loop(0, per)
        def _(i):
            arrived(ROWS_D, c * per + i)
            arrived(ROWS_C, c * per + i)

        tile = gram_tile(buf[c])
        terms = lax.dot_general(
            tile, own[:, :ds], (((0,), (0,)), ((), ())), preferred_element_type=jnp.float32
        )
        cd_out[c] = terms[2 * chunk :, :].astype(jnp.bfloat16)
        grad_copy(GRAD_CD, c).start()
        part_ab[c] = terms[: 2 * chunk, :]
        acc[...] += jnp.dot(tile, buf[c, :, :ds], preferred_element_type=jnp.float32)

    def return_b(c):
        grad_copy(GRAD_CD, c).wait_recv()
        total = part_ab[c, chunk:, :] + cd_in[c, :chunk, :].astype(jnp.float32)
        b_out[c] = total.astype(jnp.bfloat16)
        grad_copy(GRAD_B, c).start()

    def return_a(c):
        grad_copy(GRAD_B, c).wait_recv()
        total = part_ab[c, :chunk, :]
        total += jnp.where(core == 1, cd_in[c, chunk:, :].astype(jnp.float32), 0.0)
        total += jnp.where(half == 1, b_in[c].astype(jnp.float32), 0.0)
        a_out[c] = total.astype(jnp.bfloat16)
        grad_copy(GRAD_A, c).start()

    ready = per + LAG
    delays = ((tiles, ready), (return_b, ready + 1), (return_a, ready + 3))

    @pl.loop(0, (steps - 1) * per + ready + 4)
    def _(g):
        @pl.when(g < pieces)
        def _():
            forward_first(g)

        @pl.when(g < pieces - WINDOW)
        def _():
            next_own(g)

        @pl.when((g >= LAG) & (g < pieces + LAG))
        def _():
            forward_second(g - LAG)

        @pl.when(g == 1)
        def _():
            own_tile()

        for work, delay in delays:
            since = g - delay

            @pl.when((since >= 0) & (lax.rem(since + per * 8, per) == 0) & (since < pieces))
            def _():
                work(lax.div(since, per))

    @pl.loop(0, steps)
    def _(c):
        grad_copy(GRAD_A, c).wait_recv()
        total = acc[part(c), :] + a_in[c].astype(jnp.float32)
        total += jnp.where(core == 0, cd_in[c, chunk:, :].astype(jnp.float32), 0.0)
        total += jnp.where(half == 0, b_in[c].astype(jnp.float32), 0.0)
        grad = 2.0 * SIM_SCALE / (rows * n) * total
        unit = own[part(c), :ds].astype(jnp.float32)
        radial = jnp.sum(unit * grad, axis=1, keepdims=True)
        out_ref[part(c), :] = (grad - unit * radial) / length[part(c), :]

    @pl.loop(0, pieces)
    def _(g):
        sent(ROWS_C, g)
        sent(ROWS_D, g)

        @pl.when(g >= pieces - WINDOW)
        def _():
            sent(ROWS_A, g)

        @pl.when((half == 1) | (g >= pieces - WINDOW))
        def _():
            sent(ROWS_B, g)

    @pl.loop(0, steps)
    def _(c):
        for kind in (GRAD_CD, GRAD_B, GRAD_A):
            grad_copy(kind, c).wait_send()


def body(student, teacher):
    rows, ds = student.shape
    dt = teacher.shape[1]
    n = lax.axis_size("blk")
    chunk = CHUNK
    steps = rows // chunk
    wide = ds + dt
    bf16, f32 = jnp.bfloat16, jnp.float32
    flops = 2 * rows * rows * (5 * wide + 9 * ds)
    return pl.pallas_call(
        functools.partial(kernel, n, chunk, PIECE),
        out_shape=jax.ShapeDtypeStruct((rows, ds), f32),
        in_specs=[pl.BlockSpec(memory_space=pltpu.VMEM)] * 2,
        out_specs=pl.BlockSpec(memory_space=pltpu.VMEM),
        scratch_shapes=[
            pltpu.VMEM((rows, wide), bf16),
            pltpu.VMEM((rows, wide), bf16),
            pltpu.VMEM((steps, 4 * chunk, wide), bf16),
            pltpu.VMEM((rows, ds), f32),
            pltpu.VMEM((rows, 1), f32),
            pltpu.VMEM((steps, 2 * chunk, ds), f32),
            pltpu.VMEM((steps, 2 * chunk, ds), bf16),
            pltpu.VMEM((steps, 2 * chunk, ds), bf16),
            pltpu.VMEM((steps, chunk, ds), bf16),
            pltpu.VMEM((steps, chunk, ds), bf16),
            pltpu.VMEM((steps, chunk, ds), bf16),
            pltpu.VMEM((steps, chunk, ds), bf16),
            pltpu.SemaphoreType.DMA((7, rows // PIECE)),
            pltpu.SemaphoreType.DMA((7, rows // PIECE)),
        ],
        compiler_params=pltpu.CompilerParams(
            collective_id=0, has_side_effects=True, vmem_limit_bytes=56 * 1024 * 1024
        ),
        cost_estimate=pl.CostEstimate(
            flops=flops, bytes_accessed=2 * rows * wide + 4 * rows * ds, transcendentals=0
        ),
    )(student, teacher)


def solution(mesh):
    placed = (P(("groups", "blk"), None), P(("groups", "blk"), None))
    return jax.shard_map(
        body, mesh=mesh, in_specs=placed, out_specs=P(("groups", "blk"), None), check_vma=False
    )
```

```python
import functools

import jax
import jax.numpy as jnp
from jax import lax
from jax.experimental import pallas as pl
from jax.experimental.pallas import tpu as pltpu
from jax.sharding import PartitionSpec as P

SIM_SCALE = 32.0
CHUNK = 32
PIECE = 16
WINDOW = 3
LAG = 2
MESH = pl.DeviceIdType.MESH

ROWS_A, ROWS_B, ROWS_C, ROWS_D, GRAD_CD, GRAD_B, GRAD_A = range(7)


def kernel(
    n, chunk, piece, stu_ref, tea_ref, out_ref,
    own, neg, buf, acc, stu_in, tea_in, part_ab, cd_out, cd_in, b_out, b_in, a_out, a_in, send, recv, load_sem, save_sem,
):
    rows, ds = stu_ref.shape
    steps = rows // chunk
    pieces = rows // piece
    per = chunk // piece
    me = lax.axis_index("blk")
    core = lax.rem(me, 2)
    half = lax.rem(lax.div(me, 2), 2)
    up = lax.rem(me + 4, n)
    down = lax.rem(me + n - 4, n)
    side = me + 2 - 4 * half
    mate = me + 1 - 2 * core

    def part(c):
        return pl.ds(pl.multiple_of(c * chunk, chunk), chunk)

    def small(g):
        return pl.ds(pl.multiple_of(g * piece, piece), piece)

    def slot(g, kind):
        start = kind * chunk + lax.rem(g, per) * piece
        return buf.at[lax.div(g, per), pl.ds(pl.multiple_of(start, piece), piece)]

    def copy(kind, c, src, dst, to):
        return pltpu.make_async_remote_copy(
            src_ref=src, dst_ref=dst, send_sem=send.at[kind, c], recv_sem=recv.at[kind, c],
            device_id={"blk": to}, device_id_type=MESH,
        )

    def rows_copy(kind, g, src):
        to = (up, side, mate, mate)[kind]
        return copy(kind, g, src, slot(g, kind), to)

    def sent(kind, g):
        rows_copy(kind, g, own.at[small(g)]).wait_send()

    def arrived(kind, g):
        rows_copy(kind, g, own.at[small(g)]).wait_recv()

    def grad_copy(kind, c):
        src, dst, to = {
            GRAD_CD: (cd_out, cd_in, mate),
            GRAD_B: (b_out, b_in, side),
            GRAD_A: (a_out, a_in, down),
        }[kind]
        return copy(kind, c, src.at[c], dst.at[c], to)

    def loads(g):
        return (
            pltpu.make_async_copy(stu_ref.at[small(g)], stu_in.at[small(g)], load_sem.at[0, g]),
            pltpu.make_async_copy(tea_ref.at[small(g)], tea_in.at[small(g)], load_sem.at[1, g]),
        )

    def save(c):
        return pltpu.make_async_copy(acc.at[part(c)], out_ref.at[part(c)], save_sem.at[c])

    barrier = pltpu.get_barrier_semaphore()
    for other in (up, down, side, mate):
        pl.semaphore_signal(barrier, inc=1, device_id={"blk": other}, device_id_type=MESH)

    @pl.loop(0, pieces)
    def _(g):
        for load in loads(g):
            load.start()

    def normalise(g):
        here = small(g)
        for load in loads(g):
            load.wait()
        stu = stu_in[here, :].astype(jnp.float32)
        stu_len = jnp.sqrt(jnp.sum(stu * stu, axis=1, keepdims=True) + 1e-12)
        unit = (stu * (1.0 / stu_len)).astype(jnp.bfloat16)
        own[here, :ds] = unit
        neg[here, :ds] = unit
        tea = tea_in[here, :].astype(jnp.float32)
        tea_len = jnp.sqrt(jnp.sum(tea * tea, axis=1, keepdims=True) + 1e-12)
        unit = (tea * (1.0 / tea_len)).astype(jnp.bfloat16)
        own[here, ds:] = unit
        neg[here, ds:] = -unit

    def send_own(g):
        mine = own.at[small(g)]
        rows_copy(ROWS_A, g, mine).start()

        @pl.when(half == 0)
        def _():
            rows_copy(ROWS_B, g, mine).start()

        @pl.when(core == 0)
        def _():
            rows_copy(ROWS_D, g, mine).start()

    normalise(0)
    pl.semaphore_wait(barrier, 4)

    @pl.loop(0, pieces)
    def _(g):
        @pl.when(g > 0)
        def _():
            normalise(g)

        @pl.when(g < WINDOW)
        def _():
            send_own(g)

    def gram_tile(far):
        gram = lax.dot_general(
            neg[...], far, (((1,), (1,)), ((), ())), preferred_element_type=jnp.float32
        )
        return (SIM_SCALE * gram).astype(jnp.bfloat16)

    def own_tile():
        acc[...] = jnp.dot(
            gram_tile(own[...]), own[:, :ds], preferred_element_type=jnp.float32
        )

    def forward_first(g):
        arrived(ROWS_A, g)

        @pl.when(half == 1)
        def _():
            rows_copy(ROWS_B, g, slot(g, ROWS_A)).start()

        @pl.when(core == 1)
        def _():
            rows_copy(ROWS_D, g, slot(g, ROWS_A)).start()

    def forward_second(g):
        arrived(ROWS_B, g)
        rows_copy(ROWS_C, g, slot(g, ROWS_B)).start()

    def next_own(g):
        sent(ROWS_A, g)

        @pl.when(half == 0)
        def _():
            sent(ROWS_B, g)

        send_own(g + WINDOW)

    def tiles(c):
        @pl.loop(0, per)
        def _(i):
            arrived(ROWS_D, c * per + i)
            arrived(ROWS_C, c * per + i)

        tile = gram_tile(buf[c])
        terms = lax.dot_general(
            tile, own[:, :ds], (((0,), (0,)), ((), ())), preferred_element_type=jnp.float32
        )
        cd_out[c] = terms[2 * chunk :, :].astype(jnp.bfloat16)
        grad_copy(GRAD_CD, c).start()
        part_ab[c] = terms[: 2 * chunk, :]
        acc[...] += jnp.dot(tile, buf[c, :, :ds], preferred_element_type=jnp.float32)

    def return_b(c):
        grad_copy(GRAD_CD, c).wait_recv()
        total = part_ab[c, chunk:, :] + cd_in[c, :chunk, :].astype(jnp.float32)
        b_out[c] = total.astype(jnp.bfloat16)
        grad_copy(GRAD_B, c).start()

    def return_a(c):
        grad_copy(GRAD_B, c).wait_recv()
        total = part_ab[c, :chunk, :]
        total += jnp.where(core == 1, cd_in[c, chunk:, :].astype(jnp.float32), 0.0)
        total += jnp.where(half == 1, b_in[c].astype(jnp.float32), 0.0)
        a_out[c] = total.astype(jnp.bfloat16)
        grad_copy(GRAD_A, c).start()

    ready = per + LAG
    delays = ((tiles, ready), (return_b, ready + 1), (return_a, ready + 3))

    @pl.loop(0, (steps - 1) * per + ready + 4)
    def _(g):
        @pl.when(g < pieces)
        def _():
            forward_first(g)

        @pl.when(g < pieces - WINDOW)
        def _():
            next_own(g)

        @pl.when((g >= LAG) & (g < pieces + LAG))
        def _():
            forward_second(g - LAG)

        @pl.when(g == 1)
        def _():
            own_tile()

        for work, delay in delays:
            since = g - delay

            @pl.when((since >= 0) & (lax.rem(since + per * 8, per) == 0) & (since < pieces))
            def _():
                work(lax.div(since, per))

    @pl.loop(0, steps)
    def _(c):
        grad_copy(GRAD_A, c).wait_recv()
        total = acc[part(c), :] + a_in[c].astype(jnp.float32)
        total += jnp.where(core == 0, cd_in[c, chunk:, :].astype(jnp.float32), 0.0)
        total += jnp.where(half == 0, b_in[c].astype(jnp.float32), 0.0)
        acc[part(c), :] = total
        save(c).start()

    @pl.loop(0, pieces)
    def _(g):
        sent(ROWS_C, g)
        sent(ROWS_D, g)

        @pl.when(g >= pieces - WINDOW)
        def _():
            sent(ROWS_A, g)

        @pl.when((half == 1) | (g >= pieces - WINDOW))
        def _():
            sent(ROWS_B, g)

    @pl.loop(0, steps)
    def _(c):
        for kind in (GRAD_CD, GRAD_B, GRAD_A):
            grad_copy(kind, c).wait_send()
        save(c).wait()


def finish(factor, stu_ref, total_ref, out_ref):
    stu = stu_ref[...].astype(jnp.float32)
    inverse = 1.0 / jnp.sqrt(jnp.sum(stu * stu, axis=1, keepdims=True) + 1e-12)
    unit = (stu * inverse).astype(jnp.bfloat16).astype(jnp.float32)
    grad = factor * total_ref[...]
    radial = jnp.sum(unit * grad, axis=1, keepdims=True)
    out_ref[...] = (grad - unit * radial) * inverse


def body(student, teacher):
    rows, ds = student.shape
    dt = teacher.shape[1]
    n = lax.axis_size("blk")
    chunk = CHUNK
    steps = rows // chunk
    wide = ds + dt
    bf16, f32 = jnp.bfloat16, jnp.float32
    flops = 2 * rows * rows * (5 * wide + 9 * ds)
    total = pl.pallas_call(
        functools.partial(kernel, n, chunk, PIECE),
        out_shape=jax.ShapeDtypeStruct((rows, ds), f32),
        in_specs=[pl.BlockSpec(memory_space=pl.ANY)] * 2,
        out_specs=pl.BlockSpec(memory_space=pl.ANY),
        scratch_shapes=[
            pltpu.VMEM((rows, wide), bf16),
            pltpu.VMEM((rows, wide), bf16),
            pltpu.VMEM((steps, 4 * chunk, wide), bf16),
            pltpu.VMEM((rows, ds), f32),
            pltpu.VMEM((rows, ds), bf16),
            pltpu.VMEM((rows, dt), bf16),
            pltpu.VMEM((steps, 2 * chunk, ds), f32),
            pltpu.VMEM((steps, 2 * chunk, ds), bf16),
            pltpu.VMEM((steps, 2 * chunk, ds), bf16),
            pltpu.VMEM((steps, chunk, ds), bf16),
            pltpu.VMEM((steps, chunk, ds), bf16),
            pltpu.VMEM((steps, chunk, ds), bf16),
            pltpu.VMEM((steps, chunk, ds), bf16),
            pltpu.SemaphoreType.DMA((7, rows // PIECE)),
            pltpu.SemaphoreType.DMA((7, rows // PIECE)),
            pltpu.SemaphoreType.DMA((2, rows // PIECE)),
            pltpu.SemaphoreType.DMA((steps,)),
        ],
        compiler_params=pltpu.CompilerParams(
            collective_id=0, has_side_effects=True, vmem_limit_bytes=56 * 1024 * 1024
        ),
        cost_estimate=pl.CostEstimate(
            flops=flops, bytes_accessed=2 * rows * wide + 4 * rows * ds, transcendentals=0
        ),
    )(student, teacher)
    block = 128 if rows % 128 == 0 else rows
    spec = pl.BlockSpec((block, ds), lambda i: (i, 0))
    return pl.pallas_call(
        functools.partial(finish, 2.0 * SIM_SCALE / (rows * n)),
        out_shape=jax.ShapeDtypeStruct((rows, ds), f32),
        grid=(rows // block,),
        in_specs=[spec, spec],
        out_specs=spec,
        cost_estimate=pl.CostEstimate(
            flops=8 * rows * ds, bytes_accessed=10 * rows * ds, transcendentals=0
        ),
    )(student, total)


def solution(mesh):
    placed = (P(("groups", "blk"), None), P(("groups", "blk"), None))
    return jax.shard_map(
        body, mesh=mesh, in_specs=placed, out_specs=P(("groups", "blk"), None), check_vma=False
    )
```

```python
import functools

import jax
import jax.numpy as jnp
from jax import lax
from jax.experimental import pallas as pl
from jax.experimental.pallas import tpu as pltpu
from jax.sharding import PartitionSpec as P

SIM_SCALE = 32.0
CHUNK = 32
PIECE = 16
WINDOW = 3
LAG = 2
MESH = pl.DeviceIdType.MESH

ROWS_A, ROWS_B, ROWS_C, ROWS_D, GRAD_CD, GRAD_B, GRAD_A = range(7)


def kernel(
    n, chunk, piece, stu_ref, tea_ref, out_ref,
    own, neg, buf, acc, stu_in, tea_in, part_ab, cd_out, cd_in, b_out, b_in, a_out, a_in, send, recv, load_sem, save_sem, kept, extra,
):
    rows, ds = stu_ref.shape
    steps = rows // chunk
    pieces = rows // piece
    per = chunk // piece
    me = lax.axis_index("blk")
    core = lax.rem(me, 2)
    half = lax.rem(lax.div(me, 2), 2)
    up = lax.rem(me + 4, n)
    down = lax.rem(me + n - 4, n)
    side = me + 2 - 4 * half
    mate = me + 1 - 2 * core

    def part(c):
        return pl.ds(pl.multiple_of(c * chunk, chunk), chunk)

    def small(g):
        return pl.ds(pl.multiple_of(g * piece, piece), piece)

    def slot(g, kind):
        start = kind * chunk + lax.rem(g, per) * piece
        return buf.at[lax.div(g, per), pl.ds(pl.multiple_of(start, piece), piece)]

    def copy(kind, c, src, dst, to):
        return pltpu.make_async_remote_copy(
            src_ref=src, dst_ref=dst, send_sem=send.at[kind, c], recv_sem=recv.at[kind, c],
            device_id={"blk": to}, device_id_type=MESH,
        )

    def rows_copy(kind, g, src):
        to = (up, side, mate, mate)[kind]
        return copy(kind, g, src, slot(g, kind), to)

    def sent(kind, g):
        rows_copy(kind, g, own.at[small(g)]).wait_send()

    def arrived(kind, g):
        rows_copy(kind, g, own.at[small(g)]).wait_recv()

    def grad_copy(kind, c):
        src, dst, to = {
            GRAD_CD: (cd_out, cd_in, mate),
            GRAD_B: (b_out, b_in, side),
            GRAD_A: (a_out, a_in, down),
        }[kind]
        return copy(kind, c, src.at[c], dst.at[c], to)

    def loads(g):
        return (
            pltpu.make_async_copy(stu_ref.at[small(g)], stu_in.at[small(g)], load_sem.at[0, g]),
            pltpu.make_async_copy(tea_ref.at[small(g)], tea_in.at[small(g)], load_sem.at[1, g]),
        )

    def save(c):
        return pltpu.make_async_copy(acc.at[part(c)], out_ref.at[part(c)], save_sem.at[c])

    barrier = pltpu.get_barrier_semaphore()
    for other in (up, down, side, mate):
        pl.semaphore_signal(barrier, inc=1, device_id={"blk": other}, device_id_type=MESH)

    @pl.loop(0, pieces)
    def _(g):
        for load in loads(g):
            load.start()

    def normalise(g):
        here = small(g)
        for load in loads(g):
            load.wait()
        stu = stu_in[here, :].astype(jnp.float32)
        stu_len = jnp.sqrt(jnp.sum(stu * stu, axis=1, keepdims=True) + 1e-12)
        unit = (stu * (1.0 / stu_len)).astype(jnp.bfloat16)
        own[here, :ds] = unit
        neg[here, :ds] = unit
        tea = tea_in[here, :].astype(jnp.float32)
        tea_len = jnp.sqrt(jnp.sum(tea * tea, axis=1, keepdims=True) + 1e-12)
        unit = (tea * (1.0 / tea_len)).astype(jnp.bfloat16)
        own[here, ds:] = unit
        neg[here, ds:] = -unit

    def send_own(g):
        mine = own.at[small(g)]
        rows_copy(ROWS_A, g, mine).start()

        @pl.when(half == 0)
        def _():
            rows_copy(ROWS_B, g, mine).start()

        @pl.when(core == 0)
        def _():
            rows_copy(ROWS_D, g, mine).start()

    normalise(0)
    pl.semaphore_wait(barrier, 4)

    @pl.loop(0, pieces)
    def _(g):
        @pl.when(g > 0)
        def _():
            normalise(g)

        @pl.when(g < WINDOW)
        def _():
            send_own(g)

    def gram_tile(far):
        gram = lax.dot_general(
            neg[...], far, (((1,), (1,)), ((), ())), preferred_element_type=jnp.float32
        )
        return (SIM_SCALE * gram).astype(jnp.bfloat16)

    def own_tile():
        acc[...] = jnp.dot(
            gram_tile(own[...]), own[:, :ds], preferred_element_type=jnp.float32
        )

    def forward_first(g):
        arrived(ROWS_A, g)

        @pl.when((half == 1) & (g >= per))
        def _():
            rows_copy(ROWS_B, g, slot(g, ROWS_A)).start()

        @pl.when(core == 1)
        def _():
            rows_copy(ROWS_D, g, slot(g, ROWS_A)).start()

    def forward_second(g):
        arrived(ROWS_B, g)
        rows_copy(ROWS_C, g, slot(g, ROWS_B)).start()

    def next_own(g):
        sent(ROWS_A, g)

        @pl.when(half == 0)
        def _():
            sent(ROWS_B, g)

        send_own(g + WINDOW)

    def tiles(c):
        @pl.loop(0, per)
        def _(i):
            arrived(ROWS_D, c * per + i)

            @pl.when((half == 1) | (c > 0))
            def _():
                arrived(ROWS_C, c * per + i)

        @pl.when(half == 1)
        def _():
            first = buf[0, :chunk, :]
            far = buf[c, chunk : 3 * chunk, :]
            contract = (((1,), (1,)), ((), ()))
            gram = lax.dot_general(
                first[:, :ds], far[:, :ds], contract, preferred_element_type=jnp.float32
            ) - lax.dot_general(
                first[:, ds:], far[:, ds:], contract, preferred_element_type=jnp.float32
            )
            cross = (SIM_SCALE * gram).astype(jnp.bfloat16)
            kept[...] += jnp.dot(cross, far[:, :ds], preferred_element_type=jnp.float32)
            extra[...] = lax.dot_general(
                cross, first[:, :ds], (((0,), (0,)), ((), ())), preferred_element_type=jnp.float32
            )

        tile = gram_tile(buf[c])
        terms = lax.dot_general(
            tile, own[:, :ds], (((0,), (0,)), ((), ())), preferred_element_type=jnp.float32
        )
        term_c = terms[2 * chunk : 3 * chunk, :] + extra[chunk:, :]
        cd_out[c, :chunk, :] = term_c.astype(jnp.bfloat16)
        cd_out[c, chunk:, :] = terms[3 * chunk :, :].astype(jnp.bfloat16)
        grad_copy(GRAD_CD, c).start()
        part_ab[c, :chunk, :] = terms[:chunk, :]
        part_ab[c, chunk:, :] = terms[chunk : 2 * chunk, :] + extra[:chunk, :]
        acc[...] += jnp.dot(tile, buf[c, :, :ds], preferred_element_type=jnp.float32)

    def return_b(c):
        grad_copy(GRAD_CD, c).wait_recv()
        total = part_ab[c, chunk:, :] + cd_in[c, :chunk, :].astype(jnp.float32)
        b_out[c] = total.astype(jnp.bfloat16)
        grad_copy(GRAD_B, c).start()

    def return_a(c):
        grad_copy(GRAD_B, c).wait_recv()
        total = part_ab[c, :chunk, :]
        total += jnp.where(c == 0, kept[...], 0.0)
        total += jnp.where(core == 1, cd_in[c, chunk:, :].astype(jnp.float32), 0.0)
        total += jnp.where(half == 1, b_in[c].astype(jnp.float32), 0.0)
        a_out[c] = total.astype(jnp.bfloat16)
        grad_copy(GRAD_A, c).start()

    kept[...] = jnp.zeros_like(kept)
    extra[...] = jnp.zeros_like(extra)

    @pl.when(half == 0)
    def _():
        buf[0, chunk : 3 * chunk, :] = jnp.zeros((2 * chunk, buf.shape[2]), jnp.bfloat16)

    ready = per + LAG
    delays = ((tiles, ready), (return_b, ready + 1), (return_a, ready + 3))

    @pl.loop(0, (steps - 1) * per + ready + 4)
    def _(g):
        @pl.when(g < pieces)
        def _():
            forward_first(g)

        @pl.when(g < pieces - WINDOW)
        def _():
            next_own(g)

        @pl.when((g >= LAG + per * (1 - half)) & (g < pieces + LAG))
        def _():
            forward_second(g - LAG)

        @pl.when(g == 1)
        def _():
            own_tile()

        for work, delay in delays:
            since = g - delay

            @pl.when((since >= 0) & (lax.rem(since + per * 8, per) == 0) & (since < pieces))
            def _():
                if work is return_a:
                    pl.when(since > 0)(lambda: return_a(lax.div(since, per)))
                else:
                    work(lax.div(since, per))

        @pl.when(g == pieces - per + ready)
        def _():
            return_a(0)

    @pl.loop(0, steps)
    def _(c):
        grad_copy(GRAD_A, c).wait_recv()
        total = acc[part(c), :] + a_in[c].astype(jnp.float32)
        total += jnp.where(core == 0, cd_in[c, chunk:, :].astype(jnp.float32), 0.0)
        total += jnp.where(half == 0, b_in[c].astype(jnp.float32), 0.0)
        acc[part(c), :] = total
        save(c).start()

    @pl.loop(0, pieces)
    def _(g):
        sent(ROWS_D, g)

        @pl.when((half == 1) | (g >= per))
        def _():
            sent(ROWS_C, g)

        @pl.when(g >= pieces - WINDOW)
        def _():
            sent(ROWS_A, g)

        @pl.when(((half == 1) & (g >= per)) | ((half == 0) & (g >= pieces - WINDOW)))
        def _():
            sent(ROWS_B, g)

    @pl.loop(0, steps)
    def _(c):
        for kind in (GRAD_CD, GRAD_B, GRAD_A):
            grad_copy(kind, c).wait_send()
        save(c).wait()


def finish(factor, stu_ref, total_ref, out_ref):
    stu = stu_ref[...].astype(jnp.float32)
    inverse = 1.0 / jnp.sqrt(jnp.sum(stu * stu, axis=1, keepdims=True) + 1e-12)
    unit = (stu * inverse).astype(jnp.bfloat16).astype(jnp.float32)
    grad = factor * total_ref[...]
    radial = jnp.sum(unit * grad, axis=1, keepdims=True)
    out_ref[...] = (grad - unit * radial) * inverse


def body(student, teacher):
    rows, ds = student.shape
    dt = teacher.shape[1]
    n = lax.axis_size("blk")
    chunk = CHUNK
    steps = rows // chunk
    wide = ds + dt
    bf16, f32 = jnp.bfloat16, jnp.float32
    flops = 2 * rows * rows * (5 * wide + 9 * ds)
    total = pl.pallas_call(
        functools.partial(kernel, n, chunk, PIECE),
        out_shape=jax.ShapeDtypeStruct((rows, ds), f32),
        in_specs=[pl.BlockSpec(memory_space=pl.ANY)] * 2,
        out_specs=pl.BlockSpec(memory_space=pl.ANY),
        scratch_shapes=[
            pltpu.VMEM((rows, wide), bf16),
            pltpu.VMEM((rows, wide), bf16),
            pltpu.VMEM((steps, 4 * chunk, wide), bf16),
            pltpu.VMEM((rows, ds), f32),
            pltpu.VMEM((rows, ds), bf16),
            pltpu.VMEM((rows, dt), bf16),
            pltpu.VMEM((steps, 2 * chunk, ds), f32),
            pltpu.VMEM((steps, 2 * chunk, ds), bf16),
            pltpu.VMEM((steps, 2 * chunk, ds), bf16),
            pltpu.VMEM((steps, chunk, ds), bf16),
            pltpu.VMEM((steps, chunk, ds), bf16),
            pltpu.VMEM((steps, chunk, ds), bf16),
            pltpu.VMEM((steps, chunk, ds), bf16),
            pltpu.SemaphoreType.DMA((7, rows // PIECE)),
            pltpu.SemaphoreType.DMA((7, rows // PIECE)),
            pltpu.SemaphoreType.DMA((2, rows // PIECE)),
            pltpu.SemaphoreType.DMA((steps,)),
            pltpu.VMEM((chunk, ds), f32),
            pltpu.VMEM((2 * chunk, ds), f32),
        ],
        compiler_params=pltpu.CompilerParams(
            collective_id=0, has_side_effects=True, vmem_limit_bytes=56 * 1024 * 1024
        ),
        cost_estimate=pl.CostEstimate(
            flops=flops, bytes_accessed=2 * rows * wide + 4 * rows * ds, transcendentals=0
        ),
    )(student, teacher)
    block = 128 if rows % 128 == 0 else rows
    spec = pl.BlockSpec((block, ds), lambda i: (i, 0))
    return pl.pallas_call(
        functools.partial(finish, 2.0 * SIM_SCALE / (rows * n)),
        out_shape=jax.ShapeDtypeStruct((rows, ds), f32),
        grid=(rows // block,),
        in_specs=[spec, spec],
        out_specs=spec,
        cost_estimate=pl.CostEstimate(
            flops=8 * rows * ds, bytes_accessed=10 * rows * ds, transcendentals=0
        ),
    )(student, total)


def solution(mesh):
    placed = (P(("groups", "blk"), None), P(("groups", "blk"), None))
    return jax.shard_map(
        body, mesh=mesh, in_specs=placed, out_specs=P(("groups", "blk"), None), check_vma=False
    )
```
